32 devices in a mesh: tm: 4 (over y, core), chan: 8 (over z, x).
Axes of the slice: x: 2, y: 2, z: 4, core: 2. Of those that a mesh axis runs over, the one named last changes fastest.
Arguments:
- raw: bfloat16 [4096, 4096], P('tm', 'chan'), may hold values from -6 to 6
- taps: bfloat16 [512], replicated, may hold values from -0.25 to 0.25
Outputs:
- correlations: float32 [4096, 16, 1024], P('chan', 'tm')
The draws below stay inside these ranges and needn't reach their ends.
All inputs are finite; a program needn't handle non-finite values.
Results may differ from the reference program's by a relative error of at most 0.0044.
Values may be sent and summed in bfloat16 or wider, within the bound.
A program may use at most 128 MiB of HBM per device.

```python
import math
import jax
import jax.numpy as jnp
from jax import lax

C = 4096
TAPS = 512
HW = 64
FR = 1024
NT = 4096
NFRAME = 4
NSRC = 16
LAGS = 1024


def shard_levels(own_key, dims, pieces, least, largest):
    factor_of = 1.0
    for position, blocks in pieces:
        steps = jax.random.uniform(jax.random.fold_in(jax.random.fold_in(own_key, 6), position), (blocks,), jnp.float32, least / len(pieces), largest / len(pieces))
        factor_of = factor_of * jnp.repeat(jnp.exp(steps), dims[position] // blocks).reshape((-1,) + (1,) * (len(dims) - 1 - position))
    return factor_of


def centred(rng, shape, deviation, reach, split=(), kind=jnp.bfloat16):
    entries = jax.random.normal(rng, shape, jnp.float32) * deviation
    if len(split) > 0:
        entries = shard_levels(rng, shape, split, -0.22, 0.18) * entries
    return jnp.clip(entries, min=-reach, max=reach).astype(kind)


def setup_inputs(seed: int = 0) -> dict:
    splits = jax.random.split(jax.random.key(seed), 3)
    return {
        "raw": centred(splits[0], (NT, C), 1.0, 6.0, ((0, 4), (1, 8))),
        "taps": centred(splits[1], (TAPS,), TAPS ** -0.5, 0.25),
    }


epsilon = 1e-05

def reference(raw, taps):
    block = 128
    kernel = taps.astype(jnp.float32)[::-1]
    length = NT + TAPS
    kernel_spec = jnp.fft.rfft(kernel, n=length)

    def prepare(columns):
        data = columns.astype(jnp.float32)
        product = jnp.fft.rfft(data, n=length, axis=0) * kernel_spec[:, None]
        filtered = jnp.fft.irfft(product, n=length, axis=0)[:NT]
        padded = jnp.pad(jnp.abs(filtered), ((HW, HW), (0, 0)))
        total = lax.reduce_window(padded, jnp.zeros((), padded.dtype), lax.add, (2 * HW + 1, 1), (1, 1), 'VALID')
        level = total / (2 * HW + 1)
        whitened = (filtered / (level + epsilon)).astype(jnp.bfloat16)
        frames = whitened.astype(jnp.float32).reshape(NFRAME, FR, block)
        spectrum = jnp.fft.rfft(frames, n=2 * FR, axis=1)[:, :FR]
        return (jnp.real(spectrum).astype(jnp.bfloat16), jnp.imag(spectrum).astype(jnp.bfloat16))
    columns = raw.reshape(NT, C // block, block).transpose(1, 0, 2)
    spec_re, spec_im = lax.map(prepare, columns)
    stride = C // NSRC
    whole_re = spec_re.transpose(1, 2, 0, 3).reshape(NFRAME, FR, C)[:, :, ::stride].astype(jnp.float32)
    whole_im = spec_im.transpose(1, 2, 0, 3).reshape(NFRAME, FR, C)[:, :, ::stride].astype(jnp.float32)
    scale = 1.0 / math.sqrt(NFRAME * FR)
    highest = lax.Precision.HIGHEST

    def correlate(pair):
        part_re = pair[0].astype(jnp.float32)
        part_im = pair[1].astype(jnp.float32)
        real_part = jnp.einsum('bfs,bfc->csf', whole_re, part_re, precision=highest) + jnp.einsum('bfs,bfc->csf', whole_im, part_im, precision=highest)
        imag_part = jnp.einsum('bfs,bfc->csf', whole_re, part_im, precision=highest) - jnp.einsum('bfs,bfc->csf', whole_im, part_re, precision=highest)
        spectrum = lax.complex(real_part, imag_part)
        spectrum = jnp.concatenate([spectrum, jnp.zeros((block, NSRC, 1), spectrum.dtype)], axis=2)
        wave = jnp.fft.irfft(spectrum, n=2 * FR, axis=2)
        lagged = jnp.concatenate([wave[:, :, 2 * FR - LAGS // 2:], wave[:, :, :LAGS // 2]], axis=2)
        return lagged * scale
    result = lax.map(correlate, (spec_re, spec_im))
    return result.reshape(C, NSRC, LAGS)
```

```python
import functools
import math

import jax
import jax.numpy as jnp
from jax import lax
from jax.experimental import pallas as pl
from jax.experimental.pallas import tpu as pltpu
from jax.sharding import PartitionSpec as P

TAPS = 512
HW = 64
FR = 1024
SRC_DEV = 2
LAGS = 1024
EPS = 1e-05
BLK = 256
NQ = FR // BLK
MESH = pl.DeviceIdType.MESH
F32 = jnp.float32
BF16 = jnp.bfloat16


def dot(a, b):
    return lax.dot_general(a, b, (((1,), (0,)), ((), ())), preferred_element_type=F32)


def dot_nt(a, b):
    return lax.dot_general(a, b, (((1,), (1,)), ((), ())), preferred_element_type=F32)


def iota(shape, dim):
    return lax.broadcasted_iota(jnp.int32, shape, dim)


def toeplitz(row, rows):
    wide = jnp.broadcast_to(row, (rows, row.shape[1]))
    return pltpu.roll(wide, 0, 1, stride=1, stride_axis=0)


def correlate(w_at, g_ref, alt_ref, store, nframe, spd, scale):
    nyq = dot(w_at(0, nframe * FR), alt_ref[...])
    even = (iota((1, BLK), 1) % 2) == 0
    for s in range(spd):
        p = (nyq[:, s : s + 1] + nyq[:, spd + s : spd + s + 1]) * (scale / (2 * FR))
        nyquist = jnp.where(even, p, -p)
        for lb in range(LAGS // BLK):
            shift = (lb - LAGS // BLK // 2) * BLK
            lo = max(0, shift)
            hi = min(FR, FR + BLK + shift)
            acc = None
            for b in range(nframe):
                part = dot(
                    w_at(b * FR + lo, hi - lo), g_ref[s * nframe + b, lo - shift : hi - shift, :]
                )
                acc = part if acc is None else acc + part
            store(s, lb, acc * scale - nyquist)


def gather_kernel(
    n_tm, n_chan, half, rows, nchunk,
    raw_ref, taps_ref, w_ref, g_ref, alt_ref,
    raw_t, srow, srecv, rawbuf, fbuf, abuf, table, band, wsrc, ra_ref, rb_ref,
    src_send, src_recv, raw_send, raw_recv, w_send, w_recv,
):
    i = lax.axis_index("tm")
    j = lax.axis_index("chan")
    core = lax.rem(i, 2)
    kk = n_chan // n_tm
    spd = SRC_DEV * kk
    channels = 2 * half
    stride = channels // SRC_DEV
    total = n_tm * FR
    nblk = total // BLK
    home = lax.div(j, kk)
    slot = lax.rem(j, kk)

    barrier = pltpu.get_barrier_semaphore()
    for off in range(1, n_tm):
        pl.semaphore_signal(
            barrier, inc=1, device_id=(lax.rem(i + off, n_tm), j), device_id_type=MESH
        )
    for b in range(n_tm):
        for k in range(kk):
            @pl.when(jnp.logical_or(i != b, j != i * kk + k))
            def _():
                pl.semaphore_signal(
                    barrier, inc=1, device_id=(b, i * kk + k), device_id_type=MESH
                )

    pick = (iota((8, channels), 1) == iota((8, channels), 0) * stride).astype(BF16)
    cols = dot_nt(pick, raw_ref[...])
    for c in range(SRC_DEV):
        for q in range(NQ):
            srow[c * NQ + q : c * NQ + q + 1, :] = cols[c : c + 1, q * BLK : (q + 1) * BLK]

    def turn(block):
        raw_t[block * 128 : (block + 1) * 128, :] = raw_ref[:, block * 128 : (block + 1) * 128].T

    def raw_copy(off, k):
        peer = lax.rem(i + off, n_tm)
        return pltpu.make_async_remote_copy(
            src_ref=raw_t.at[pl.ds(pl.multiple_of(lax.rem(peer, 2) * half + k * rows, 16), rows), :],
            dst_ref=rawbuf.at[
                pl.ds(k * rows, rows), pl.ds(pl.multiple_of(TAPS + i * FR, 128), FR)
            ],
            send_sem=raw_send.at[off, k],
            recv_sem=raw_recv.at[off, k],
            device_id=(peer, j),
            device_id_type=MESH,
        )

    def src_copy(peer):
        return pltpu.make_async_remote_copy(
            src_ref=srow,
            dst_ref=srecv.at[i, slot],
            send_sem=src_send.at[peer],
            recv_sem=src_recv.at[i, slot],
            device_id=(home, peer),
            device_id_type=MESH,
        )

    turned = set()
    for k in range(nchunk):
        for h in range(2):
            first = (h * half + k * rows) // 128
            last = (h * half + (k + 1) * rows - 1) // 128
            for block in range(first, last + 1):
                if block not in turned:
                    turned.add(block)
                    turn(block)
        if k == 0:
            pl.semaphore_wait(barrier, n_tm - 1 + n_chan - jnp.where(home == i, 1, 0))
            for peer in range(n_chan):
                @pl.when(jnp.logical_or(home != i, peer != j))
                def _():
                    src_copy(peer).start()
        for off in range(1, n_tm):
            raw_copy(off, k).start()

    @pl.when(home == i)
    def _():
        srecv[i, slot] = srow[...]

    rawbuf[:, :TAPS] = jnp.zeros((half, TAPS), BF16)
    rawbuf[:, pl.ds(pl.multiple_of(TAPS + i * FR, 128), FR)] = raw_t[
        pl.ds(pl.multiple_of(core * half, 16), half), :
    ]
    abuf[:, : BLK // 2] = jnp.zeros((rows, BLK // 2), BF16)
    abuf[:, BLK // 2 + total :] = jnp.zeros((rows, BLK // 2), BF16)

    table[...] = toeplitz(taps_ref[...], BLK).T.astype(BF16)
    gap = iota((2 * BLK, BLK), 0) - BLK // 2 - iota((2 * BLK, BLK), 1)
    band[...] = (jnp.abs(gap) <= HW).astype(BF16)

    def whiten(f, window):
        return (f / (window * (1.0 / (2 * HW + 1)) + EPS)).astype(BF16)

    for b in range(n_tm):
        for k in range(kk):
            @pl.when(jnp.logical_or(i != b, j != i * kk + k))
            def _():
                pltpu.make_async_remote_copy(
                    src_ref=srow,
                    dst_ref=srecv.at[b, k],
                    send_sem=src_send.at[0],
                    recv_sem=src_recv.at[b, k],
                    device_id=(b, i * kk + k),
                    device_id_type=MESH,
                ).wait_recv()
    now, one, two = [], [], []
    for k in range(kk):
        for c in range(SRC_DEV):
            block = jnp.concatenate(
                [srecv[b, k, c * NQ : (c + 1) * NQ, :] for b in range(n_tm)], axis=0
            )
            now.append(block)
            one.append(jnp.concatenate([jnp.zeros((1, BLK), F32), block[:-1]], axis=0))
            two.append(jnp.concatenate([jnp.zeros((2, BLK), F32), block[:-2]], axis=0))
    x = jnp.concatenate([jnp.concatenate(p, axis=0) for p in (two, one, now)], axis=1)
    f = dot(x.astype(BF16), table[...])
    mag = jnp.abs(f)
    before, after = [], []
    for s in range(spd):
        part = mag[s * nblk : (s + 1) * nblk]
        before.append(jnp.concatenate([jnp.zeros((1, BLK // 2), F32), part[:-1, BLK // 2 :]], 0))
        after.append(jnp.concatenate([part[1:, : BLK // 2], jnp.zeros((1, BLK // 2), F32)], 0))
    around = jnp.concatenate(
        [jnp.concatenate(before, 0), mag, jnp.concatenate(after, 0)], axis=1
    )
    white = whiten(f, dot(around.astype(BF16), band[...]))
    kdim = iota((BLK, BLK), 0)
    mdim = iota((BLK, BLK), 1)
    ra_ref[...] = dot(white, jnp.logical_and(kdim == 0, mdim == 0).astype(BF16))
    rb_ref[...] = dot(white, (kdim + mdim == BLK).astype(BF16))
    sign = jnp.where(iota((8, BLK), 1) % 2 == 0, 1.0, -1.0).astype(BF16)
    sums = dot_nt(sign, white)
    for b in range(n_tm):
        r = iota((spd * nblk, 128), 0)
        lane = iota((spd * nblk, 128), 1)
        inside = jnp.logical_and(r // nblk == lane % spd, (r % nblk) // NQ == b)
        inside = jnp.logical_and(inside, lane < 2 * spd).astype(F32)
        ns = lax.dot_general(
            sums, inside, (((1,), (0,)), ((), ())),
            precision=lax.Precision.HIGHEST, preferred_element_type=F32,
        )[0:1]
        head = ns.astype(BF16).astype(F32)
        ns = jnp.where(iota((1, 128), 1) < spd, head, ns - head)
        flip = jnp.where(iota((FR, 128), 0) % 2 == 0, ns, -ns)
        alt_ref[b * FR : (b + 1) * FR, :] = flip.astype(BF16)

    def build(n, carry):
        row = n * NQ

        def rev(q):
            value = jnp.zeros((1, BLK), F32)
            if q < NQ:
                value = value + ra_ref[pl.ds(row + q, 1), :]
            if 1 <= q <= NQ:
                value = value + rb_ref[pl.ds(row + q - 1, 1), :]
            return value

        pieces = [rev(q) for q in range(NQ + 2)]
        for d in range(NQ + 1):
            base = jnp.concatenate([pieces[d], pieces[d + 1]], axis=1)
            g_ref[n, d * BLK : (d + 1) * BLK, :] = toeplitz(base, BLK)[:, :BLK].astype(BF16)
        return carry

    lax.fori_loop(0, spd * n_tm, build, 0)

    def w_copy(k):
        at = pl.ds(pl.multiple_of(core * half + k * rows, 16), rows)
        return pltpu.make_async_remote_copy(
            src_ref=w_ref.at[at, :],
            dst_ref=w_ref.at[at, :],
            send_sem=w_send.at[k],
            recv_sem=w_recv.at[k],
            device_id=(i + 1 - 2 * core, j),
            device_id_type=MESH,
        )

    def whiten_chunk(k):
        for off in range(1, n_tm):
            sender = lax.rem(i + n_tm - off, n_tm)
            pltpu.make_async_remote_copy(
                src_ref=raw_t.at[pl.ds(0, rows), :],
                dst_ref=rawbuf.at[
                    pl.ds(k * rows, rows), pl.ds(pl.multiple_of(TAPS + sender * FR, 128), FR)
                ],
                send_sem=raw_send.at[off, k],
                recv_sem=raw_recv.at[off, k],
                device_id=(sender, j),
                device_id_type=MESH,
            ).wait_recv()

        def fir(n, carry):
            t = pl.multiple_of(n * BLK, BLK)
            f = dot(rawbuf[k * rows : (k + 1) * rows, pl.ds(t, TAPS + BLK)], table[...])
            fbuf[:, pl.ds(t, BLK)] = f
            abuf[:, pl.ds(pl.multiple_of(t + BLK // 2, 128), BLK)] = jnp.abs(f).astype(BF16)
            return carry

        lax.fori_loop(0, nblk, fir, 0)

        def norm(n, carry):
            t = pl.multiple_of(n * BLK, BLK)
            window = dot(abuf[:, pl.ds(t, 2 * BLK)], band[...])
            at = pl.ds(pl.multiple_of(core * half + k * rows, 16), rows)
            w_ref[at, pl.ds(t, BLK)] = whiten(fbuf[:, pl.ds(t, BLK)], window)
            return carry

        lax.fori_loop(0, nblk, norm, 0)
        w_copy(k).start()

    for k in range(nchunk):
        whiten_chunk(k)
    for k in range(nchunk):
        at = pl.ds(pl.multiple_of((1 - core) * half + k * rows, 16), rows)
        pltpu.make_async_remote_copy(
            src_ref=w_ref.at[at, :],
            dst_ref=w_ref.at[at, :],
            send_sem=w_send.at[k],
            recv_sem=w_recv.at[k],
            device_id=(i + 1 - 2 * core, j),
            device_id_type=MESH,
        ).wait_recv()
        w_copy(k).wait_send()
        for off in range(1, n_tm):
            raw_copy(off, k).wait_send()
    for peer in range(n_chan):
        @pl.when(jnp.logical_or(home != i, peer != j))
        def _():
            src_copy(peer).wait_send()


def finish_kernel(nframe, spd, scale, tile, w_ref, g_ref, alt_ref, out_ref):
    at = pl.ds(pl.multiple_of(pl.program_id(0) * tile, tile), tile)

    def w_at(start, size):
        return w_ref[at, start : start + size]

    def store(s, lb, value):
        out_ref[:, s, lb * BLK : (lb + 1) * BLK] = value

    correlate(w_at, g_ref, alt_ref, store, nframe, spd, scale)


def on_device(raw, taps):
    samples, channels = raw.shape
    n_tm = lax.axis_size("tm")
    n_chan = lax.axis_size("chan")
    half = channels // 2
    rows = min(64, half)
    nchunk = half // rows
    spd = SRC_DEV * n_chan // n_tm
    total = samples * n_tm
    nblk = total // BLK
    scale = 1.0 / math.sqrt(total)
    row = jnp.pad(taps.astype(F32), (1, BLK - 1))[None]
    vmem = pl.BlockSpec(memory_space=pltpu.VMEM)
    dma = pltpu.SemaphoreType.DMA
    tile = min(128, channels)
    kept = 2 * (channels * total + spd * n_tm * (FR + BLK) * BLK + total * 128)
    on_chip = kept <= 36 * 2**20
    limit = (24 if on_chip else 60) * 2**20
    hold = pltpu.VMEM if on_chip else jax.ShapeDtypeStruct
    w, g, alt = pl.pallas_call(
        functools.partial(gather_kernel, n_tm, n_chan, half, rows, nchunk),
        out_shape=(
            hold((channels, total), BF16),
            hold((spd * n_tm, FR + BLK, BLK), BF16),
            hold((total, 128), BF16),
        ),
        in_specs=[vmem, vmem],
        out_specs=(vmem, vmem, vmem),
        scratch_shapes=[
            pltpu.VMEM((channels, FR), BF16),
            pltpu.VMEM((SRC_DEV * NQ, BLK), F32),
            pltpu.VMEM((n_tm, n_chan // n_tm, SRC_DEV * NQ, BLK), F32),
            pltpu.VMEM((half, TAPS + total), BF16),
            pltpu.VMEM((rows, total), F32),
            pltpu.VMEM((rows, total + BLK), BF16),
            pltpu.VMEM((TAPS + BLK, BLK), BF16),
            pltpu.VMEM((2 * BLK, BLK), BF16),
            pltpu.VMEM((8, BLK), BF16),
            pltpu.VMEM((spd * nblk, BLK), F32),
            pltpu.VMEM((spd * nblk, BLK), F32),
            dma((n_chan,)),
            dma((n_tm, n_chan // n_tm)),
            dma((n_tm, nchunk)),
            dma((n_tm, nchunk)),
            dma((nchunk,)),
            dma((nchunk,)),
        ],
        compiler_params=pltpu.CompilerParams(
            collective_id=0, has_side_effects=True, vmem_limit_bytes=limit
        ),
    )(raw, row)
    return pl.pallas_call(
        functools.partial(finish_kernel, n_tm, spd, scale, tile),
        out_shape=jax.ShapeDtypeStruct((channels, spd, LAGS), F32),
        grid=(channels // tile,),
        in_specs=[
            vmem,
            vmem,
            vmem,
        ],
        out_specs=pl.BlockSpec((tile, spd, LAGS), lambda c: (c, 0, 0)),
        compiler_params=pltpu.CompilerParams(vmem_limit_bytes=limit),
    )(w, g, alt)


def solution(mesh):
    placed = (P("tm", "chan"), P())
    return jax.shard_map(
        on_device, mesh=mesh, in_specs=placed, out_specs=P("chan", "tm", None), check_vma=False
    )
```

```python
import functools
import math

import jax
import jax.numpy as jnp
from jax import lax
from jax.experimental import pallas as pl
from jax.experimental.pallas import tpu as pltpu
from jax.sharding import PartitionSpec as P

TAPS = 512
HW = 64
FR = 1024
SRC_DEV = 2
LAGS = 1024
EPS = 1e-05
BLK = 256
LANE = 128
NQ = FR // BLK
MESH = pl.DeviceIdType.MESH
F32 = jnp.float32
BF16 = jnp.bfloat16


def dot(a, b):
    return lax.dot_general(a, b, (((1,), (0,)), ((), ())), preferred_element_type=F32)


def dot_nt(a, b):
    return lax.dot_general(a, b, (((1,), (1,)), ((), ())), preferred_element_type=F32)


def iota(shape, dim):
    return lax.broadcasted_iota(jnp.int32, shape, dim)


def toeplitz(row, rows, first=0):
    wide = jnp.broadcast_to(row, (rows, row.shape[1]))
    return pltpu.roll(wide, first, 1, stride=1, stride_axis=0)


def correlate(w_at, g_ref, alt_ref, store, nframe, spd, scale):
    nyq = dot(w_at(0, nframe * FR), alt_ref[...])
    even = (iota((1, BLK), 1) % 2) == 0
    for s in range(spd):
        p = (nyq[:, s : s + 1] + nyq[:, spd + s : spd + s + 1]) * (scale / (2 * FR))
        nyquist = jnp.where(even, p, -p)
        for lb in range(LAGS // BLK):
            shift = (lb - LAGS // BLK // 2) * BLK
            lo = max(0, shift)
            hi = min(FR, FR + BLK + shift)
            acc = None
            for b in range(nframe):
                part = dot(
                    w_at(b * FR + lo, hi - lo), g_ref[s * nframe + b, lo - shift : hi - shift, :]
                )
                acc = part if acc is None else acc + part
            store(s, lb, acc * scale - nyquist)


def chunk_of(w_ref, k, half, rows):
    def w_at(start, size):
        return jnp.concatenate(
            [w_ref[h * half + k * rows : h * half + (k + 1) * rows, start : start + size] for h in (0, 1)],
            axis=0,
        )

    return w_at


def gather_kernel(
    n_tm, n_chan, half, rows, nchunk, scale,
    raw_ref, taps_ref, w_ref, g_ref, alt_ref, part_ref,
    raw_t, srow, srecv, rawbuf, fbuf, abuf, table, band, wsrc, ra_ref, rb_ref,
    src_send, src_recv, raw_send, raw_recv, w_send, w_recv,
):
    i = lax.axis_index("tm")
    j = lax.axis_index("chan")
    core = lax.rem(i, 2)
    kk = n_chan // n_tm
    spd = SRC_DEV * kk
    channels = 2 * half
    stride = channels // SRC_DEV
    total = n_tm * FR
    nblk = total // BLK
    group = math.gcd(nblk, 16)
    home = lax.div(j, kk)
    slot = lax.rem(j, kk)

    barrier = pltpu.get_barrier_semaphore()
    for off in range(1, n_tm):
        pl.semaphore_signal(
            barrier, inc=1, device_id=(lax.rem(i + off, n_tm), j), device_id_type=MESH
        )
    for b in range(n_tm):
        for k in range(kk):
            @pl.when(jnp.logical_or(i != b, j != i * kk + k))
            def _():
                pl.semaphore_signal(
                    barrier, inc=1, device_id=(b, i * kk + k), device_id_type=MESH
                )

    pick = (iota((8, channels), 1) == iota((8, channels), 0) * stride).astype(BF16)
    cols = dot_nt(pick, raw_ref[...])
    for c in range(SRC_DEV):
        for q in range(NQ):
            srow[c * NQ + q : c * NQ + q + 1, :] = cols[c : c + 1, q * BLK : (q + 1) * BLK]

    def turn(block):
        raw_t[block * 128 : (block + 1) * 128, :] = raw_ref[:, block * 128 : (block + 1) * 128].T

    def raw_copy(off, k):
        peer = lax.rem(i + off, n_tm)
        return pltpu.make_async_remote_copy(
            src_ref=raw_t.at[pl.ds(pl.multiple_of(lax.rem(peer, 2) * half + k * rows, 16), rows), :],
            dst_ref=rawbuf.at[
                pl.ds(k * rows, rows), pl.ds(pl.multiple_of(TAPS + i * FR, 128), FR)
            ],
            send_sem=raw_send.at[off, k],
            recv_sem=raw_recv.at[off, k],
            device_id=(peer, j),
            device_id_type=MESH,
        )

    def src_copy(peer):
        return pltpu.make_async_remote_copy(
            src_ref=srow,
            dst_ref=srecv.at[i, slot],
            send_sem=src_send.at[peer],
            recv_sem=src_recv.at[i, slot],
            device_id=(home, peer),
            device_id_type=MESH,
        )

    turned = set()
    for k in range(nchunk):
        for h in range(2):
            first = (h * half + k * rows) // 128
            last = (h * half + (k + 1) * rows - 1) // 128
            for block in range(first, last + 1):
                if block not in turned:
                    turned.add(block)
                    turn(block)
        if k == 0:
            pl.semaphore_wait(barrier, n_tm - 1 + n_chan - jnp.where(home == i, 1, 0))
            for peer in range(n_chan):
                @pl.when(jnp.logical_or(home != i, peer != j))
                def _():
                    src_copy(peer).start()
        for off in range(1, n_tm):
            raw_copy(off, k).start()

    @pl.when(home == i)
    def _():
        srecv[i, slot] = srow[...]

    rawbuf[:, :TAPS] = jnp.zeros((half, TAPS), BF16)
    rawbuf[:, pl.ds(pl.multiple_of(TAPS + i * FR, 128), FR)] = raw_t[
        pl.ds(pl.multiple_of(core * half, 16), half), :
    ]
    abuf[:, : BLK // 2] = jnp.zeros((rows, BLK // 2), BF16)
    abuf[:, BLK // 2 + total :] = jnp.zeros((rows, BLK // 2), BF16)

    line = jnp.concatenate([taps_ref[...].astype(F32), jnp.zeros((1, BLK), F32)], axis=1)
    table[...] = toeplitz(line, BLK, 1).T.astype(BF16)
    gap = iota((2 * BLK, BLK), 0) - BLK // 2 - iota((2 * BLK, BLK), 1)
    band[...] = (jnp.abs(gap) <= HW).astype(BF16)

    def whiten(f, window):
        return (f / (window * (1.0 / (2 * HW + 1)) + EPS)).astype(BF16)

    for b in range(n_tm):
        for k in range(kk):
            @pl.when(jnp.logical_or(i != b, j != i * kk + k))
            def _():
                pltpu.make_async_remote_copy(
                    src_ref=srow,
                    dst_ref=srecv.at[b, k],
                    send_sem=src_send.at[0],
                    recv_sem=src_recv.at[b, k],
                    device_id=(b, i * kk + k),
                    device_id_type=MESH,
                ).wait_recv()
    now, one, two = [], [], []
    for k in range(kk):
        for c in range(SRC_DEV):
            block = jnp.concatenate(
                [srecv[b, k, c * NQ : (c + 1) * NQ, :] for b in range(n_tm)], axis=0
            )
            now.append(block)
            one.append(jnp.concatenate([jnp.zeros((1, BLK), F32), block[:-1]], axis=0))
            two.append(jnp.concatenate([jnp.zeros((2, BLK), F32), block[:-2]], axis=0))
    x = jnp.concatenate([jnp.concatenate(p, axis=0) for p in (two, one, now)], axis=1)
    f = dot(x.astype(BF16), table[...])
    mag = jnp.abs(f)
    before, after = [], []
    for s in range(spd):
        part = mag[s * nblk : (s + 1) * nblk]
        before.append(jnp.concatenate([jnp.zeros((1, BLK // 2), F32), part[:-1, BLK // 2 :]], 0))
        after.append(jnp.concatenate([part[1:, : BLK // 2], jnp.zeros((1, BLK // 2), F32)], 0))
    around = jnp.concatenate(
        [jnp.concatenate(before, 0), mag, jnp.concatenate(after, 0)], axis=1
    )
    white = whiten(f, dot(around.astype(BF16), band[...]))
    kdim = iota((BLK, BLK), 0)
    mdim = iota((BLK, BLK), 1)
    same = kdim // LANE == mdim // LANE
    ra_ref[...] = dot(white, jnp.logical_and(kdim == mdim, mdim % LANE == 0).astype(BF16))
    rb_ref[...] = dot(
        white, jnp.logical_and(same, kdim % LANE + mdim % LANE == LANE).astype(BF16)
    )
    sign = jnp.where(iota((8, BLK), 1) % 2 == 0, 1.0, -1.0).astype(BF16)
    sums = dot_nt(sign, white)
    for b in range(n_tm):
        r = iota((spd * nblk, 128), 0)
        lane = iota((spd * nblk, 128), 1)
        inside = jnp.logical_and(r // nblk == lane % spd, (r % nblk) // NQ == b)
        inside = jnp.logical_and(inside, lane < 2 * spd).astype(F32)
        ns = lax.dot_general(
            sums, inside, (((1,), (0,)), ((), ())),
            precision=lax.Precision.HIGHEST, preferred_element_type=F32,
        )[0:1]
        head = ns.astype(BF16).astype(F32)
        ns = jnp.where(iota((1, 128), 1) < spd, head, ns - head)
        flip = jnp.where(iota((FR, 128), 0) % 2 == 0, ns, -ns)
        alt_ref[b * FR : (b + 1) * FR, :] = flip.astype(BF16)

    def build(n, carry):
        row = n * NQ

        def rev(q):
            value = jnp.zeros((1, LANE), F32)
            if q < FR // LANE:
                at = q % 2 * LANE
                value = value + ra_ref[pl.ds(row + q // 2, 1), :][:, at : at + LANE]
            if 1 <= q <= FR // LANE:
                at = (q - 1) % 2 * LANE
                value = value + rb_ref[pl.ds(row + (q - 1) // 2, 1), :][:, at : at + LANE]
            return value

        pieces = [rev(q) for q in range(FR // LANE + 2)]
        g_ref[n, :LANE, LANE:] = jnp.zeros((LANE, LANE), BF16)
        g_ref[n, FR + LANE :, :LANE] = jnp.zeros((LANE, LANE), BF16)
        for d in range(FR // LANE + 1):
            base = jnp.concatenate([pieces[d], pieces[d + 1]], axis=1)
            tile = toeplitz(base, LANE)[:, :LANE].astype(BF16)
            g_ref[n, d * LANE : (d + 1) * LANE, :LANE] = tile
            g_ref[n, (d + 1) * LANE : (d + 2) * LANE, LANE:] = tile
        return carry

    def w_copy(k):
        at = pl.ds(pl.multiple_of(core * half + k * rows, 16), rows)
        return pltpu.make_async_remote_copy(
            src_ref=w_ref.at[at, :],
            dst_ref=w_ref.at[at, :],
            send_sem=w_send.at[k],
            recv_sem=w_recv.at[k],
            device_id=(i + 1 - 2 * core, j),
            device_id_type=MESH,
        )

    def whiten_chunk(k):
        for off in range(1, n_tm):
            sender = lax.rem(i + n_tm - off, n_tm)
            pltpu.make_async_remote_copy(
                src_ref=raw_t.at[pl.ds(0, rows), :],
                dst_ref=rawbuf.at[
                    pl.ds(k * rows, rows), pl.ds(pl.multiple_of(TAPS + sender * FR, 128), FR)
                ],
                send_sem=raw_send.at[off, k],
                recv_sem=raw_recv.at[off, k],
                device_id=(sender, j),
                device_id_type=MESH,
            ).wait_recv()

        def fir(n, carry):
            start = pl.multiple_of(n * group * BLK, BLK)
            x = jnp.concatenate(
                [
                    rawbuf[k * rows : (k + 1) * rows, pl.ds(start + t * BLK, TAPS + BLK)]
                    for t in range(group)
                ],
                axis=0,
            )
            f = dot(x, table[...])
            mag = jnp.abs(f).astype(BF16)
            for t in range(group):
                part = slice(t * rows, (t + 1) * rows)
                fbuf[:, pl.ds(start + t * BLK, BLK)] = f[part]
                abuf[:, pl.ds(start + t * BLK + BLK // 2, BLK)] = mag[part]
            return carry

        def norm(n, carry):
            start = pl.multiple_of(n * group * BLK, BLK)
            x = jnp.concatenate(
                [abuf[:, pl.ds(start + t * BLK, 2 * BLK)] for t in range(group)], axis=0
            )
            window = dot(x, band[...])
            at = pl.ds(pl.multiple_of(core * half + k * rows, 16), rows)
            for t in range(group):
                part = slice(t * rows, (t + 1) * rows)
                w_ref[at, pl.ds(start + t * BLK, BLK)] = whiten(
                    fbuf[:, pl.ds(start + t * BLK, BLK)], window[part]
                )
            return carry

        if nblk == group:
            fir(0, 0)
            norm(0, 0)
        else:
            lax.fori_loop(0, nblk // group, fir, 0)
            lax.fori_loop(0, nblk // group, norm, 0)
        w_copy(k).start()

    def w_arrival(k):
        at = pl.ds(pl.multiple_of((1 - core) * half + k * rows, 16), rows)
        pltpu.make_async_remote_copy(
            src_ref=w_ref.at[at, :],
            dst_ref=w_ref.at[at, :],
            send_sem=w_send.at[k],
            recv_sem=w_recv.at[k],
            device_id=(i + 1 - 2 * core, j),
            device_id_type=MESH,
        ).wait_recv()

    def correlate_chunk(k):
        w_arrival(k)

        def store(s, lb, value):
            part_ref[2 * k * rows : 2 * (k + 1) * rows, s, lb * BLK : (lb + 1) * BLK] = value

        correlate(chunk_of(w_ref, k, half, rows), g_ref, alt_ref, store, n_tm, spd, scale)

    count = spd * n_tm
    lax.fori_loop(0, count // 2, build, 0)
    whiten_chunk(0)
    lax.fori_loop(count // 2, count, build, 0)
    for k in range(nchunk - 1):
        if k == 0:
            correlate_chunk(0)
            whiten_chunk(1)
        else:
            whiten_chunk(k + 1)
            correlate_chunk(k)
    w_arrival(nchunk - 1)
    for k in range(nchunk):
        w_copy(k).wait_send()
        for off in range(1, n_tm):
            raw_copy(off, k).wait_send()
    for peer in range(n_chan):
        @pl.when(jnp.logical_or(home != i, peer != j))
        def _():
            src_copy(peer).wait_send()


def finish_kernel(
    nframe, spd, scale, half, rows, nchunk, w_ref, g_ref, alt_ref, part_ref, out_ref, last, sems
):
    def out_copy(k, h):
        row = h * half + k * rows
        if k < nchunk - 1:
            src = part_ref.at[pl.ds((2 * k + h) * rows, rows)]
        else:
            src = last.at[pl.ds(h * rows, rows)]
        return pltpu.make_async_copy(src, out_ref.at[pl.ds(row, rows)], sems.at[k, h])

    for k in range(nchunk - 1):
        for h in (0, 1):
            out_copy(k, h).start()

    def store(s, lb, value):
        last[:, s, lb * BLK : (lb + 1) * BLK] = value

    correlate(chunk_of(w_ref, nchunk - 1, half, rows), g_ref, alt_ref, store, nframe, spd, scale)
    for h in (0, 1):
        out_copy(nchunk - 1, h).start()
    for k in range(nchunk):
        for h in (0, 1):
            out_copy(k, h).wait()


def on_device(raw, taps):
    samples, channels = raw.shape
    n_tm = lax.axis_size("tm")
    n_chan = lax.axis_size("chan")
    half = channels // 2
    rows = min(64, half)
    nchunk = half // rows
    spd = SRC_DEV * n_chan // n_tm
    total = samples * n_tm
    nblk = total // BLK
    scale = 1.0 / math.sqrt(total)
    vmem = pl.BlockSpec(memory_space=pltpu.VMEM)
    dma = pltpu.SemaphoreType.DMA
    part_shape = (max((nchunk - 1) * 2 * rows, 8), spd, LAGS)
    kept = 2 * (channels * total + spd * n_tm * (FR + BLK) * BLK + total * 128)
    kept += 4 * math.prod(part_shape)
    on_chip = kept <= 36 * 2**20
    limit = (24 if on_chip else 60) * 2**20
    hold = pltpu.VMEM if on_chip else jax.ShapeDtypeStruct
    w, g, alt, part = pl.pallas_call(
        functools.partial(gather_kernel, n_tm, n_chan, half, rows, nchunk, scale),
        out_shape=(
            hold((channels, total), BF16),
            hold((spd * n_tm, FR + BLK, BLK), BF16),
            hold((total, 128), BF16),
            hold(part_shape, F32),
        ),
        in_specs=[vmem, vmem],
        out_specs=(vmem, vmem, vmem, vmem),
        scratch_shapes=[
            pltpu.VMEM((channels, FR), BF16),
            pltpu.VMEM((SRC_DEV * NQ, BLK), F32),
            pltpu.VMEM((n_tm, n_chan // n_tm, SRC_DEV * NQ, BLK), F32),
            pltpu.VMEM((half, TAPS + total), BF16),
            pltpu.VMEM((rows, total), F32),
            pltpu.VMEM((rows, total + BLK), BF16),
            pltpu.VMEM((TAPS + BLK, BLK), BF16),
            pltpu.VMEM((2 * BLK, BLK), BF16),
            pltpu.VMEM((8, BLK), BF16),
            pltpu.VMEM((spd * nblk, BLK), F32),
            pltpu.VMEM((spd * nblk, BLK), F32),
            dma((n_chan,)),
            dma((n_tm, n_chan // n_tm)),
            dma((n_tm, nchunk)),
            dma((n_tm, nchunk)),
            dma((nchunk,)),
            dma((nchunk,)),
        ],
        compiler_params=pltpu.CompilerParams(
            collective_id=0, has_side_effects=True, vmem_limit_bytes=limit
        ),
    )(raw, taps[None])
    return pl.pallas_call(
        functools.partial(finish_kernel, n_tm, spd, scale, half, rows, nchunk),
        out_shape=jax.ShapeDtypeStruct((channels, spd, LAGS), F32),
        in_specs=[vmem, vmem, vmem, vmem],
        out_specs=pl.BlockSpec(memory_space=pl.ANY),
        scratch_shapes=[pltpu.VMEM((2 * rows, spd, LAGS), F32), dma((nchunk, 2))],
        compiler_params=pltpu.CompilerParams(vmem_limit_bytes=limit),
    )(w, g, alt, part)


def solution(mesh):
    placed = (P("tm", "chan"), P())
    return jax.shard_map(
        on_device, mesh=mesh, in_specs=placed, out_specs=P("chan", "tm", None), check_vma=False
    )
```

```python
import functools
import math

import jax
import jax.numpy as jnp
from jax import lax
from jax.experimental import pallas as pl
from jax.experimental.pallas import tpu as pltpu
from jax.sharding import PartitionSpec as P

TAPS = 512
HW = 64
FR = 1024
SRC_DEV = 2
LAGS = 1024
EPS = 1e-05
BLK = 256
LANE = 128
NQ = FR // BLK
MESH = pl.DeviceIdType.MESH
F32 = jnp.float32
BF16 = jnp.bfloat16


def dot(a, b):
    return lax.dot_general(a, b, (((1,), (0,)), ((), ())), preferred_element_type=F32)


def dot_nt(a, b):
    return lax.dot_general(a, b, (((1,), (1,)), ((), ())), preferred_element_type=F32)


def iota(shape, dim):
    return lax.broadcasted_iota(jnp.int32, shape, dim)


def toeplitz(row, rows, first=0):
    wide = jnp.broadcast_to(row, (rows, row.shape[1]))
    return pltpu.roll(wide, first, 1, stride=1, stride_axis=0)


def correlate(w_at, g_ref, alt_ref, store, nframe, spd, scale):
    nyq = dot(w_at(0, nframe * FR), alt_ref[...])
    even = (iota((1, BLK), 1) % 2) == 0
    for s in range(spd):
        p = (nyq[:, s : s + 1] + nyq[:, spd + s : spd + s + 1]) * (scale / (2 * FR))
        nyquist = jnp.where(even, p, -p)
        for lb in range(LAGS // BLK):
            shift = (lb - LAGS // BLK // 2) * BLK
            lo = max(0, shift)
            hi = min(FR, FR + BLK + shift)
            acc = None
            for b in range(nframe):
                part = dot(
                    w_at(b * FR + lo, hi - lo), g_ref[s * nframe + b, lo - shift : hi - shift, :]
                )
                acc = part if acc is None else acc + part
            store(s, lb, acc * scale - nyquist)


def chunk_of(w_ref, k, half, rows):
    def w_at(start, size):
        return jnp.concatenate(
            [w_ref[h * half + k * rows : h * half + (k + 1) * rows, start : start + size] for h in (0, 1)],
            axis=0,
        )

    return w_at


def gather_kernel(
    n_tm, n_chan, half, rows, nchunk, scale,
    raw_hbm, taps_ref, w_ref, g_ref, alt_ref, part_ref,
    raw_ref, fetched, raw_t, srow, srecv, rawbuf, fbuf, abuf, table, band, wsrc, ra_ref, rb_ref,
    src_send, src_recv, raw_send, raw_recv, w_send, w_recv,
):
    i = lax.axis_index("tm")
    j = lax.axis_index("chan")
    core = lax.rem(i, 2)
    kk = n_chan // n_tm
    spd = SRC_DEV * kk
    channels = 2 * half
    stride = channels // SRC_DEV
    total = n_tm * FR
    nblk = total // BLK
    group = math.gcd(nblk, 16)
    home = lax.div(j, kk)
    slot = lax.rem(j, kk)

    barrier = pltpu.get_barrier_semaphore()
    for off in range(1, n_tm):
        pl.semaphore_signal(
            barrier, inc=1, device_id=(lax.rem(i + off, n_tm), j), device_id_type=MESH
        )
    for b in range(n_tm):
        for k in range(kk):
            @pl.when(jnp.logical_or(i != b, j != i * kk + k))
            def _():
                pl.semaphore_signal(
                    barrier, inc=1, device_id=(b, i * kk + k), device_id_type=MESH
                )

    def fetch(block):
        at = pl.ds(block * LANE, LANE)
        return pltpu.make_async_copy(raw_hbm.at[:, at], raw_ref.at[:, at], fetched.at[block])

    def source_rows(c):
        first = c * stride // LANE * LANE
        pick = (iota((8, LANE), 1) == c * stride - first).astype(BF16)
        cols = dot_nt(pick, raw_ref[:, first : first + LANE])
        for q in range(NQ):
            srow[c * NQ + q : c * NQ + q + 1, :] = cols[0:1, q * BLK : (q + 1) * BLK]

    def turn(block):
        fetch(block).wait()
        raw_t[block * 128 : (block + 1) * 128, :] = raw_ref[:, block * 128 : (block + 1) * 128].T

    def raw_copy(off, k):
        peer = lax.rem(i + off, n_tm)
        return pltpu.make_async_remote_copy(
            src_ref=raw_t.at[pl.ds(pl.multiple_of(lax.rem(peer, 2) * half + k * rows, 16), rows), :],
            dst_ref=rawbuf.at[
                pl.ds(k * rows, rows), pl.ds(pl.multiple_of(TAPS + i * FR, 128), FR)
            ],
            send_sem=raw_send.at[off, k],
            recv_sem=raw_recv.at[off, k],
            device_id=(peer, j),
            device_id_type=MESH,
        )

    def src_copy(peer):
        return pltpu.make_async_remote_copy(
            src_ref=srow,
            dst_ref=srecv.at[i, slot],
            send_sem=src_send.at[peer],
            recv_sem=src_recv.at[i, slot],
            device_id=(home, peer),
            device_id_type=MESH,
        )

    blocks = channels // LANE
    for block in sorted(range(blocks), key=lambda n: n % max(blocks // 2, 1)):
        fetch(block).start()
    turned = set()
    for k in range(nchunk):
        for h in range(2):
            first = (h * half + k * rows) // 128
            last = (h * half + (k + 1) * rows - 1) // 128
            for block in range(first, last + 1):
                if block not in turned:
                    turned.add(block)
                    turn(block)
        if k == 0:
            for c in range(SRC_DEV):
                source_rows(c)
            pl.semaphore_wait(barrier, n_tm - 1 + n_chan - jnp.where(home == i, 1, 0))
            for peer in range(n_chan):
                @pl.when(jnp.logical_or(home != i, peer != j))
                def _():
                    src_copy(peer).start()
        for off in range(1, n_tm):
            raw_copy(off, k).start()

    @pl.when(home == i)
    def _():
        srecv[i, slot] = srow[...]

    rawbuf[:, :TAPS] = jnp.zeros((half, TAPS), BF16)
    rawbuf[:, pl.ds(pl.multiple_of(TAPS + i * FR, 128), FR)] = raw_t[
        pl.ds(pl.multiple_of(core * half, 16), half), :
    ]
    abuf[:, : BLK // 2] = jnp.zeros((rows, BLK // 2), BF16)
    abuf[:, BLK // 2 + total :] = jnp.zeros((rows, BLK // 2), BF16)

    line = jnp.concatenate([taps_ref[...].astype(F32), jnp.zeros((1, BLK), F32)], axis=1)
    table[...] = toeplitz(line, BLK, 1).T.astype(BF16)
    gap = iota((2 * BLK, BLK), 0) - BLK // 2 - iota((2 * BLK, BLK), 1)
    band[...] = (jnp.abs(gap) <= HW).astype(BF16)

    def whiten(f, window):
        return (f / (window * (1.0 / (2 * HW + 1)) + EPS)).astype(BF16)

    for b in range(n_tm):
        for k in range(kk):
            @pl.when(jnp.logical_or(i != b, j != i * kk + k))
            def _():
                pltpu.make_async_remote_copy(
                    src_ref=srow,
                    dst_ref=srecv.at[b, k],
                    send_sem=src_send.at[0],
                    recv_sem=src_recv.at[b, k],
                    device_id=(b, i * kk + k),
                    device_id_type=MESH,
                ).wait_recv()
    now, one, two = [], [], []
    for k in range(kk):
        for c in range(SRC_DEV):
            block = jnp.concatenate(
                [srecv[b, k, c * NQ : (c + 1) * NQ, :] for b in range(n_tm)], axis=0
            )
            now.append(block)
            one.append(jnp.concatenate([jnp.zeros((1, BLK), F32), block[:-1]], axis=0))
            two.append(jnp.concatenate([jnp.zeros((2, BLK), F32), block[:-2]], axis=0))
    x = jnp.concatenate([jnp.concatenate(p, axis=0) for p in (two, one, now)], axis=1)
    f = dot(x.astype(BF16), table[...])
    mag = jnp.abs(f)
    before, after = [], []
    for s in range(spd):
        part = mag[s * nblk : (s + 1) * nblk]
        before.append(jnp.concatenate([jnp.zeros((1, BLK // 2), F32), part[:-1, BLK // 2 :]], 0))
        after.append(jnp.concatenate([part[1:, : BLK // 2], jnp.zeros((1, BLK // 2), F32)], 0))
    around = jnp.concatenate(
        [jnp.concatenate(before, 0), mag, jnp.concatenate(after, 0)], axis=1
    )
    white = whiten(f, dot(around.astype(BF16), band[...]))
    kdim = iota((BLK, BLK), 0)
    mdim = iota((BLK, BLK), 1)
    same = kdim // LANE == mdim // LANE
    ra_ref[...] = dot(white, jnp.logical_and(kdim == mdim, mdim % LANE == 0).astype(BF16))
    rb_ref[...] = dot(
        white, jnp.logical_and(same, kdim % LANE + mdim % LANE == LANE).astype(BF16)
    )
    sign = jnp.where(iota((8, BLK), 1) % 2 == 0, 1.0, -1.0).astype(BF16)
    sums = dot_nt(sign, white)
    for b in range(n_tm):
        r = iota((spd * nblk, 128), 0)
        lane = iota((spd * nblk, 128), 1)
        inside = jnp.logical_and(r // nblk == lane % spd, (r % nblk) // NQ == b)
        inside = jnp.logical_and(inside, lane < 2 * spd).astype(F32)
        ns = lax.dot_general(
            sums, inside, (((1,), (0,)), ((), ())),
            precision=lax.Precision.HIGHEST, preferred_element_type=F32,
        )[0:1]
        head = ns.astype(BF16).astype(F32)
        ns = jnp.where(iota((1, 128), 1) < spd, head, ns - head)
        flip = jnp.where(iota((FR, 128), 0) % 2 == 0, ns, -ns)
        alt_ref[b * FR : (b + 1) * FR, :] = flip.astype(BF16)

    def build(n, carry):
        row = n * NQ

        def rev(q):
            value = jnp.zeros((1, LANE), F32)
            if q < FR // LANE:
                at = q % 2 * LANE
                value = value + ra_ref[pl.ds(row + q // 2, 1), :][:, at : at + LANE]
            if 1 <= q <= FR // LANE:
                at = (q - 1) % 2 * LANE
                value = value + rb_ref[pl.ds(row + (q - 1) // 2, 1), :][:, at : at + LANE]
            return value

        pieces = [rev(q) for q in range(FR // LANE + 2)]
        g_ref[n, :LANE, LANE:] = jnp.zeros((LANE, LANE), BF16)
        g_ref[n, FR + LANE :, :LANE] = jnp.zeros((LANE, LANE), BF16)
        for d in range(FR // LANE + 1):
            base = jnp.concatenate([pieces[d], pieces[d + 1]], axis=1)
            tile = toeplitz(base, LANE)[:, :LANE].astype(BF16)
            g_ref[n, d * LANE : (d + 1) * LANE, :LANE] = tile
            g_ref[n, (d + 1) * LANE : (d + 2) * LANE, LANE:] = tile
        return carry

    def w_copy(k):
        at = pl.ds(pl.multiple_of(core * half + k * rows, 16), rows)
        return pltpu.make_async_remote_copy(
            src_ref=w_ref.at[at, :],
            dst_ref=w_ref.at[at, :],
            send_sem=w_send.at[k],
            recv_sem=w_recv.at[k],
            device_id=(i + 1 - 2 * core, j),
            device_id_type=MESH,
        )

    def whiten_chunk(k):
        for off in range(1, n_tm):
            sender = lax.rem(i + n_tm - off, n_tm)
            pltpu.make_async_remote_copy(
                src_ref=raw_t.at[pl.ds(0, rows), :],
                dst_ref=rawbuf.at[
                    pl.ds(k * rows, rows), pl.ds(pl.multiple_of(TAPS + sender * FR, 128), FR)
                ],
                send_sem=raw_send.at[off, k],
                recv_sem=raw_recv.at[off, k],
                device_id=(sender, j),
                device_id_type=MESH,
            ).wait_recv()

        def fir(n, carry):
            start = pl.multiple_of(n * group * BLK, BLK)
            x = jnp.concatenate(
                [
                    rawbuf[k * rows : (k + 1) * rows, pl.ds(start + t * BLK, TAPS + BLK)]
                    for t in range(group)
                ],
                axis=0,
            )
            f = dot(x, table[...])
            mag = jnp.abs(f).astype(BF16)
            for t in range(group):
                part = slice(t * rows, (t + 1) * rows)
                fbuf[:, pl.ds(start + t * BLK, BLK)] = f[part]
                abuf[:, pl.ds(start + t * BLK + BLK // 2, BLK)] = mag[part]
            return carry

        def norm(n, carry):
            start = pl.multiple_of(n * group * BLK, BLK)
            x = jnp.concatenate(
                [abuf[:, pl.ds(start + t * BLK, 2 * BLK)] for t in range(group)], axis=0
            )
            window = dot(x, band[...])
            at = pl.ds(pl.multiple_of(core * half + k * rows, 16), rows)
            for t in range(group):
                part = slice(t * rows, (t + 1) * rows)
                w_ref[at, pl.ds(start + t * BLK, BLK)] = whiten(
                    fbuf[:, pl.ds(start + t * BLK, BLK)], window[part]
                )
            return carry

        if nblk == group:
            fir(0, 0)
            norm(0, 0)
        else:
            lax.fori_loop(0, nblk // group, fir, 0)
            lax.fori_loop(0, nblk // group, norm, 0)
        w_copy(k).start()

    def w_arrival(k):
        at = pl.ds(pl.multiple_of((1 - core) * half + k * rows, 16), rows)
        pltpu.make_async_remote_copy(
            src_ref=w_ref.at[at, :],
            dst_ref=w_ref.at[at, :],
            send_sem=w_send.at[k],
            recv_sem=w_recv.at[k],
            device_id=(i + 1 - 2 * core, j),
            device_id_type=MESH,
        ).wait_recv()

    def correlate_chunk(k):
        w_arrival(k)

        def store(s, lb, value):
            part_ref[2 * k * rows : 2 * (k + 1) * rows, s, lb * BLK : (lb + 1) * BLK] = value

        correlate(chunk_of(w_ref, k, half, rows), g_ref, alt_ref, store, n_tm, spd, scale)

    count = spd * n_tm
    lax.fori_loop(0, count // 2, build, 0)
    whiten_chunk(0)
    lax.fori_loop(count // 2, count, build, 0)
    for k in range(nchunk - 1):
        if k == 0:
            correlate_chunk(0)
            whiten_chunk(1)
        else:
            whiten_chunk(k + 1)
            correlate_chunk(k)
    w_arrival(nchunk - 1)
    for k in range(nchunk):
        w_copy(k).wait_send()
        for off in range(1, n_tm):
            raw_copy(off, k).wait_send()
    for peer in range(n_chan):
        @pl.when(jnp.logical_or(home != i, peer != j))
        def _():
            src_copy(peer).wait_send()


def finish_kernel(
    nframe, spd, scale, half, rows, nchunk, w_ref, g_ref, alt_ref, part_ref, out_ref, last, sems
):
    def out_copy(k, h):
        row = h * half + k * rows
        if k < nchunk - 1:
            src = part_ref.at[pl.ds((2 * k + h) * rows, rows)]
        else:
            src = last.at[pl.ds(h * rows, rows)]
        return pltpu.make_async_copy(src, out_ref.at[pl.ds(row, rows)], sems.at[k, h])

    for k in range(nchunk - 1):
        for h in (0, 1):
            out_copy(k, h).start()

    def store(s, lb, value):
        last[:, s, lb * BLK : (lb + 1) * BLK] = value

    correlate(chunk_of(w_ref, nchunk - 1, half, rows), g_ref, alt_ref, store, nframe, spd, scale)
    for h in (0, 1):
        out_copy(nchunk - 1, h).start()
    for k in range(nchunk):
        for h in (0, 1):
            out_copy(k, h).wait()


def on_device(raw, taps):
    samples, channels = raw.shape
    n_tm = lax.axis_size("tm")
    n_chan = lax.axis_size("chan")
    half = channels // 2
    rows = min(64, half)
    nchunk = half // rows
    spd = SRC_DEV * n_chan // n_tm
    total = samples * n_tm
    nblk = total // BLK
    scale = 1.0 / math.sqrt(total)
    vmem = pl.BlockSpec(memory_space=pltpu.VMEM)
    dma = pltpu.SemaphoreType.DMA
    part_shape = (max((nchunk - 1) * 2 * rows, 8), spd, LAGS)
    kept = 2 * (channels * total + spd * n_tm * (FR + BLK) * BLK + total * 128)
    kept += 4 * math.prod(part_shape)
    on_chip = kept <= 36 * 2**20
    limit = (24 if on_chip else 60) * 2**20
    hold = pltpu.VMEM if on_chip else jax.ShapeDtypeStruct
    w, g, alt, part = pl.pallas_call(
        functools.partial(gather_kernel, n_tm, n_chan, half, rows, nchunk, scale),
        out_shape=(
            hold((channels, total), BF16),
            hold((spd * n_tm, FR + BLK, BLK), BF16),
            hold((total, 128), BF16),
            hold(part_shape, F32),
        ),
        in_specs=[pl.BlockSpec(memory_space=pltpu.HBM), vmem],
        out_specs=(vmem, vmem, vmem, vmem),
        scratch_shapes=[
            pltpu.VMEM((samples, channels), BF16),
            dma((channels // LANE,)),
            pltpu.VMEM((channels, FR), BF16),
            pltpu.VMEM((SRC_DEV * NQ, BLK), F32),
            pltpu.VMEM((n_tm, n_chan // n_tm, SRC_DEV * NQ, BLK), F32),
            pltpu.VMEM((half, TAPS + total), BF16),
            pltpu.VMEM((rows, total), F32),
            pltpu.VMEM((rows, total + BLK), BF16),
            pltpu.VMEM((TAPS + BLK, BLK), BF16),
            pltpu.VMEM((2 * BLK, BLK), BF16),
            pltpu.VMEM((8, BLK), BF16),
            pltpu.VMEM((spd * nblk, BLK), F32),
            pltpu.VMEM((spd * nblk, BLK), F32),
            dma((n_chan,)),
            dma((n_tm, n_chan // n_tm)),
            dma((n_tm, nchunk)),
            dma((n_tm, nchunk)),
            dma((nchunk,)),
            dma((nchunk,)),
        ],
        compiler_params=pltpu.CompilerParams(
            collective_id=0, has_side_effects=True, vmem_limit_bytes=limit
        ),
    )(raw, taps[None])
    return pl.pallas_call(
        functools.partial(finish_kernel, n_tm, spd, scale, half, rows, nchunk),
        out_shape=jax.ShapeDtypeStruct((channels, spd, LAGS), F32),
        in_specs=[vmem, vmem, vmem, vmem],
        out_specs=pl.BlockSpec(memory_space=pl.ANY),
        scratch_shapes=[pltpu.VMEM((2 * rows, spd, LAGS), F32), dma((nchunk, 2))],
        compiler_params=pltpu.CompilerParams(vmem_limit_bytes=limit),
    )(w, g, alt, part)


def solution(mesh):
    placed = (P("tm", "chan"), P())
    return jax.shard_map(
        on_device, mesh=mesh, in_specs=placed, out_specs=P("chan", "tm", None), check_vma=False
    )
```
